256 devices in a mesh: section: 8 (over z), sp: 8 (over y, x_hi), prompt: 4 (over x_lo, core).
Axes of the slice: x: 4 (x_hi: 2, x_lo: 2; x = x_hi * 2 + x_lo), y: 4, z: 8, core: 2. Of those that a mesh axis runs over, the one named last changes fastest.
Arguments:
- latents: bfloat16 [32, 64, 3072], P('prompt', 'sp'), parts along dimension 0, may hold values from -6 to 6
- offsets: int32 [32], P('prompt'), parts along dimension 0, may hold values from 0 to 448, as said below
- norm_gain: float32 [8, 3072], P('section'), may hold values from 0.5 to 2
- w_qkv: bfloat16 [8, 3072, 3, 2048], P('section', None, None, 'sp'), may hold values from -0.109375 to 0.109375
- qk_gain: float32 [8, 2, 128], P('section'), may hold values from 0.5 to 2
- w_out: bfloat16 [8, 2048, 3072], P('section', 'sp'), may hold values from -0.125 to 0.125
- kv_cache: bfloat16 [8, 2, 2048, 2048], P('section', None, 'prompt', 'sp'), parts along dimension 2, may hold values from -24 to 24
Outputs:
- section_out: bfloat16 [8, 32, 64, 3072], P('section', 'prompt', 'sp'), parts along dimension 1
- kv_out: bfloat16 [8, 2, 2048, 2048], P('section', None, 'prompt', 'sp'), parts along dimension 2
The draws below stay inside these ranges and needn't reach their ends.
There are 4 independent parts, one for each index of `prompt`. The reference program is written for one: setup_inputs(seed, part) draws one part's arguments, and reference() takes and returns one part's arrays. A program takes and returns all parts, laid end to end along the dimension named above; an argument that names none is the same for every part. Nothing has to cross between parts.
Inputs may be any that keep to these rules, and one draw needn't show every extreme that they name: `offsets`: each multiple of 64 below 512 appears once.
All inputs are finite; a program needn't handle non-finite values.
Results may differ from the reference program's by a relative error of at most 0.04.
Values may be sent and summed in bfloat16 or wider, within the bound.
No kernel may reach another device: no remote copies, remote signals or barrier semaphores. Data moves between devices by JAX's collectives and lax.ppermute only.
A program may use at most 64 MiB of HBM per device.

```python
import math
import jax
import jax.numpy as jnp
from jax import lax

D = 3072
HEADS = 16
HEAD_DIM = 128
PATCHES = 8
PATCH = 64
SEQ = 512
SECTIONS = 8
N_SECTION = 8
N_SP = 8


def draw_offsets(key, part):
    key = jax.random.fold_in(key, 1)
    return (jax.random.permutation(key, PATCHES) * PATCH).astype(jnp.int32)


def draw_qk_gain(key, part):
    key = jax.random.fold_in(key, 2)
    shape = (SECTIONS, 2, HEAD_DIM)
    gains = jnp.exp(jax.random.uniform(key, shape, jnp.float32, math.log(0.5), math.log(2.0)))
    return gains.astype(jnp.float32)


def draw_kv_cache(key, part):
    key = jax.random.fold_in(key, 3)
    first_key = jax.random.fold_in(key, 0)
    shape = (SECTIONS, 2, SEQ, HEADS * HEAD_DIM)
    values = jax.random.normal(first_key, shape, jnp.float32)
    return jnp.clip(values, -24.0, 24.0).astype(jnp.bfloat16)


def steps_of(key, extent, shards, low, high):
    factor_of = 1.0
    for position, blocks in shards:
        heights = jax.random.uniform(jax.random.fold_in(jax.random.fold_in(key, 6), position), (blocks,), jnp.float32, low / len(shards), high / len(shards))
        factor_of = factor_of * jnp.repeat(jnp.exp(heights), extent[position] // blocks).reshape((-1,) + (1,) * (len(extent) - 1 - position))
    return factor_of


def centred(key, dims, scale, reach, shards=(), dtype=jnp.bfloat16):
    result = scale * jax.random.normal(key, dims, jnp.float32)
    if shards:
        result = result * steps_of(key, dims, shards, -0.22, 0.18)
    return jnp.clip(result, -reach, reach).astype(dtype)


def setup_inputs(seed: int = 0, part: int = 0) -> dict:
    streams_of = jax.random.split(jax.random.key(seed), 8)
    part_keys = jax.random.split(jax.random.fold_in(streams_of[7], part), 8)
    return {
        "latents": centred(part_keys[0], (PATCHES, PATCH, D), 1.0, 6.0, ((1, 8),)),
        "offsets": draw_offsets(jax.random.fold_in(jax.random.fold_in(streams_of[7], part), 71), part),
        "norm_gain": jnp.clip(jnp.exp(math.log(2.0) - 1.3862944 * jax.random.uniform(streams_of[2], (SECTIONS, D), jnp.float32) ** steps_of(streams_of[2], (SECTIONS, D), ((0, 8),), -0.2, 0.2)), 0.5, 2.0),
        "w_qkv": centred(streams_of[3], (SECTIONS, D, 3, HEADS * HEAD_DIM), D ** -0.5, 0.109375, ((0, 8), (3, 8))),
        "qk_gain": draw_qk_gain(jax.random.fold_in(streams_of[7], 71), part),
        "w_out": centred(streams_of[5], (SECTIONS, HEADS * HEAD_DIM, D), (HEADS * HEAD_DIM) ** -0.5, 0.125, ((0, 8), (1, 8))),
        "kv_cache": draw_kv_cache(jax.random.fold_in(jax.random.fold_in(streams_of[7], part), 71), part),
    }


EPS = 1e-06

def rms_scale(values):
    return values * lax.rsqrt(lax.optimization_barrier(jnp.mean(values * values, axis=-1, keepdims=True)) + EPS)

def block_step(inflow, offset, kv_state, gain_row, w_project, gains, w_output):
    inflow32 = inflow.astype(jnp.float32)
    normed = (rms_scale(inflow32) * gain_row).astype(jnp.bfloat16)
    projected = jnp.dot(normed, w_project.reshape(D, 3 * HEADS * HEAD_DIM), preferred_element_type=jnp.float32)
    projected = projected.reshape(PATCH, 3, HEADS, HEAD_DIM)
    queries = (rms_scale(projected[:, 0]) * gains[0]).astype(jnp.bfloat16)
    keys_new = (rms_scale(projected[:, 1]) * gains[1]).astype(jnp.bfloat16)
    values_new = projected[:, 2].astype(jnp.bfloat16)
    fresh_kv = jnp.stack([keys_new, values_new]).reshape(2, PATCH, HEADS * HEAD_DIM)
    kv_state = lax.dynamic_update_slice(kv_state, fresh_kv, (jnp.int32(0), offset.astype(jnp.int32), jnp.int32(0)))
    key_rows = kv_state[0].reshape(SEQ, HEADS, HEAD_DIM).astype(jnp.float32)
    value_rows = kv_state[1].reshape(SEQ, HEADS, HEAD_DIM).astype(jnp.float32)
    scores = jnp.einsum('phd,shd->hps', queries.astype(jnp.float32), key_rows) / math.sqrt(HEAD_DIM)
    weights = jax.nn.softmax(scores, axis=-1).astype(jnp.bfloat16)
    mixture = jnp.einsum('hps,shd->phd', weights.astype(jnp.float32), value_rows).astype(jnp.bfloat16)
    grouped = mixture.reshape(PATCH, N_SP, HEADS * HEAD_DIM // N_SP).astype(jnp.float32)
    out_groups = w_output.reshape(N_SP, HEADS * HEAD_DIM // N_SP, D).astype(jnp.float32)
    group_terms = jnp.einsum('pgk,gkd->gpd', grouped, out_groups).astype(jnp.bfloat16)
    group_terms = lax.optimization_barrier(group_terms).astype(jnp.float32)
    attended = lax.optimization_barrier(jnp.sum(group_terms, axis=0))
    return (kv_state, (inflow32 + attended).astype(jnp.bfloat16))

def reference(latents, offsets, norm_gain, w_qkv, qk_gain, w_out, kv_cache):
    hidden = latents
    patch_order = offsets // PATCH
    section_list = []
    cache_list = []
    for section_no in range(N_SECTION):

        def visit_patch(kv_state, offset, section_no=section_no, hidden=hidden):
            patch_index = offset // PATCH
            inflow = lax.dynamic_index_in_dim(hidden, patch_index, 0, keepdims=False)
            return block_step(inflow, offset, kv_state, norm_gain[section_no], w_qkv[section_no], qk_gain[section_no], w_out[section_no])
        kv_state, results = lax.scan(visit_patch, kv_cache[section_no], offsets)
        hidden = jnp.zeros_like(hidden).at[patch_order].set(results)
        section_list.append(hidden)
        cache_list.append(kv_state)
    return (jnp.stack(section_list), jnp.stack(cache_list))
```

```python
import math

import jax
import jax.numpy as jnp
from jax import lax
from jax.experimental import pallas as pl
from jax.experimental.pallas import tpu as pltpu
from jax.sharding import PartitionSpec as P

EPS = 1e-06
CHUNK = 2
OUT_BLOCK = 512
MIB = 1024 * 1024
BF16, F32 = jnp.bfloat16, jnp.float32
VMEM = pl.BlockSpec(memory_space=pltpu.VMEM)
SMEM = pl.BlockSpec(memory_space=pltpu.SMEM)


def onward(value, steps=1):
    count = lax.axis_size("section")
    return lax.ppermute(value, "section", [(i, (i + steps) % count) for i in range(count)])


def spread(value):
    count = lax.axis_size("sp")
    copies = jnp.broadcast_to(value[None], (count,) + value.shape)
    return lax.all_to_all(copies, "sp", 0, 0)


def cost(macs, size):
    return pl.CostEstimate(flops=2 * macs, bytes_accessed=size, transcendentals=0)


def order_kernel(patch_rows, plan, latents, ordered):
    for j in range(latents.shape[0]):
        ordered[j] = latents[plan[j] // patch_rows]


def order_call(patch_rows, plan, latents):
    return pl.pallas_call(
        lambda *refs: order_kernel(patch_rows, *refs),
        out_shape=jax.ShapeDtypeStruct(latents.shape, latents.dtype),
        in_specs=[SMEM, VMEM],
        out_specs=VMEM,
        compiler_params=pltpu.CompilerParams(vmem_limit_bytes=4 * MIB),
    )(plan, latents)


def block_kernel(tick, sections, patch_rows, entry, projects, finishes, *refs):
    refs = list(refs)
    plan, gain, qk_gain, w_project, kv_in, kept_in = refs[:6]
    del refs[:6]
    if projects:
        gathered, x_before, w_before = refs[:3]
        del refs[:3]
    if entry is not None:
        first = refs.pop(0)
    if finishes:
        w_last = refs.pop(0)
    x_out, mixture_out, kv_out, kept_out = refs[:4]
    del refs[:4]
    if finishes:
        terms_out = refs.pop(0)
    normed, x_wide = refs[:2]
    rows, width = x_out.shape
    local_width = kv_out.shape[2]
    head_dim = qk_gain.shape[1]
    chunks = kept_out.shape[0]
    shard_rows = kept_out.shape[2]
    patches = chunks * CHUNK
    section_no, group_no = plan[patches], plan[patches + 1]
    blocks = [slice(i, i + OUT_BLOCK) for i in range(0, width, OUT_BLOCK)]

    kv_out[...] = kv_in[...]
    kept_out[...] = kept_in[...]
    if projects:
        mixed = refs[2]
        for i in range(gathered.shape[0]):
            mixed[:, i * local_width : (i + 1) * local_width] = gathered[i]
        for cols in blocks:
            attended = jnp.dot(mixed[...], w_before[:, cols], preferred_element_type=F32)
            x = x_before[:, cols].astype(F32) + attended
            x_wide[:, cols] = x.astype(BF16).astype(F32)
        block_kept = jnp.where(section_no == 0, sections, section_no)
        slot_kept = tick - block_kept

        @pl.when((slot_kept >= 0) & (slot_kept < chunks))
        def _():
            for i in range(CHUNK):
                at = pl.multiple_of(i * patch_rows + group_no * shard_rows, shard_rows)
                kept_out[slot_kept, i] = x_wide[pl.ds(at, shard_rows), :].astype(BF16)

    def enter():
        for i in range(CHUNK):
            for g in range(first.shape[0]):
                at = i * patch_rows + g * shard_rows
                x_wide[at : at + shard_rows, :] = first[g, entry + i].astype(F32)

    if entry is not None:
        if projects:
            pl.when(section_no == 0)(enter)
        else:
            enter()

    squares = jnp.zeros((rows, 1), F32)
    for cols in blocks:
        x = x_wide[:, cols]
        squares += jnp.sum(x * x, axis=-1, keepdims=True)
        x_out[:, cols] = x.astype(BF16)
    scale = lax.rsqrt(squares / width + EPS)
    for cols in blocks:
        normed[:, cols] = (x_wide[:, cols] * scale * gain[:, cols]).astype(BF16)

    def projected(i):
        return jnp.dot(normed[...], w_project[i], preferred_element_type=F32)

    def head_norm(values, gains):
        parts = []
        for h in range(local_width // head_dim):
            part = values[:, h * head_dim : (h + 1) * head_dim]
            part = part * lax.rsqrt(jnp.mean(part * part, axis=-1, keepdims=True) + EPS)
            parts.append((part * gains).astype(BF16))
        return parts

    queries = head_norm(projected(0), qk_gain[0:1, :])
    keys_new = jnp.concatenate(head_norm(projected(1), qk_gain[1:2, :]), axis=1)
    values_new = projected(2).astype(BF16)
    slot = tick - section_no
    active = (slot >= 0) & (slot < chunks)
    turn = jnp.clip(slot, 0, chunks - 1) * CHUNK
    for i in range(CHUNK):
        part = slice(i * patch_rows, (i + 1) * patch_rows)
        place = pl.ds(pl.multiple_of(plan[turn + i], patch_rows), patch_rows)

        @pl.when(active)
        def _():
            kv_out[0, place, :] = keys_new[part]
            kv_out[1, place, :] = values_new[part]

        for h in range(local_width // head_dim):
            cols = slice(h * head_dim, (h + 1) * head_dim)
            scores = lax.dot_general(
                queries[h][part], kv_out[0, :, cols], (((1,), (1,)), ((), ())),
                preferred_element_type=F32,
            ) * (1.0 / math.sqrt(head_dim))
            weights = jnp.exp(scores - jnp.max(scores, axis=-1, keepdims=True))
            weights = weights / jnp.sum(weights, axis=-1, keepdims=True)
            mixture = jnp.dot(
                weights.astype(BF16), kv_out[1, :, cols], preferred_element_type=F32
            )
            mixture_out[part, cols] = mixture.astype(BF16)
    if finishes:
        for cols in blocks:
            terms = jnp.dot(mixture_out[...], w_last[:, cols], preferred_element_type=F32)
            for i in range(CHUNK):
                for g in range(terms_out.shape[0]):
                    at = i * patch_rows + g * shard_rows
                    terms_out[g, i, :, cols] = terms[at : at + shard_rows].astype(BF16)


def block_call(tick, sections, patch_rows, plan, gain, qk_gain, w_project, kv_state, kept,
               before=(), first=(), entry=None, last=()):
    width = gain.shape[1]
    local_width = kv_state.shape[2]
    rows = CHUNK * patch_rows
    macs = rows * width * local_width * 3
    out_shape = [
        jax.ShapeDtypeStruct((rows, width), BF16),
        jax.ShapeDtypeStruct((rows, local_width), BF16),
        jax.ShapeDtypeStruct(kv_state.shape, kv_state.dtype),
        jax.ShapeDtypeStruct(kept.shape, kept.dtype),
    ]
    if last:
        out_shape.append(
            jax.ShapeDtypeStruct((patch_rows // kept.shape[2],) + kept.shape[1:], BF16)
        )
    scratch = [pltpu.VMEM((rows, width), BF16), pltpu.VMEM((rows, width), F32)]
    if before:
        full = before[2].shape[0]
        macs += rows * width * full
        scratch.append(pltpu.VMEM((rows, full), BF16))
    operands = (gain, qk_gain, w_project, kv_state, kept, *before, *first, *last)
    return pl.pallas_call(
        lambda *refs: block_kernel(
            tick, sections, patch_rows, entry, bool(before), bool(last), *refs
        ),
        out_shape=out_shape,
        in_specs=[SMEM] + [VMEM] * len(operands),
        out_specs=[VMEM] * len(out_shape),
        scratch_shapes=scratch,
        compiler_params=pltpu.CompilerParams(vmem_limit_bytes=10 * MIB),
        cost_estimate=cost(macs, 2 * macs // rows),
    )(plan, *operands)


def close_kernel(sections, patch_rows, plan, terms, own, results, section_out):
    patches = section_out.shape[0]
    section_no = plan[patches]
    chunks = results.shape[0]
    for j in range(patches):
        section_out[plan[j] // patch_rows] = results[j // CHUNK, j % CHUNK]

    @pl.when(section_no == sections - 1)
    def _():
        for i in range(CHUNK):
            total = own[i].astype(F32)
            for g in range(terms.shape[0]):
                total += terms[g, i].astype(F32)
            section_out[plan[patches - CHUNK + i] // patch_rows] = total.astype(BF16)


def close_call(sections, patch_rows, plan, terms, own, results, shape):
    return pl.pallas_call(
        lambda *refs: close_kernel(sections, patch_rows, *refs),
        out_shape=jax.ShapeDtypeStruct(shape, BF16),
        in_specs=[SMEM, VMEM, VMEM, VMEM],
        out_specs=VMEM,
        compiler_params=pltpu.CompilerParams(vmem_limit_bytes=6 * MIB),
    )(plan, terms, own, results)


def on_device(latents, offsets, norm_gain, w_qkv, qk_gain, w_out, kv_cache):
    groups = lax.axis_size("sp")
    sections = lax.axis_size("section")
    section_no = lax.axis_index("section")
    group_no = lax.axis_index("sp")
    prompt_no = lax.axis_index("prompt")
    prompts = lax.axis_size("prompt")
    patches, shard_rows, width = latents.shape
    patch_rows = shard_rows * groups
    local_width = w_out.shape[1]
    chunks = patches // CHUNK
    plan = jnp.concatenate([offsets, jnp.stack([section_no, group_no]).astype(jnp.int32)])

    share = local_width // prompts
    own_share = lax.dynamic_slice_in_dim(w_out[0], prompt_no * share, share, 0)
    w_before = lax.all_gather(onward(own_share), ("sp", "prompt"), axis=0, tiled=True)
    w_project = jnp.swapaxes(w_qkv[0], 0, 1)

    ordered = order_call(patch_rows, plan, latents)
    entering = spread(ordered[:CHUNK])
    kv_state = kv_cache[0]
    kept = jnp.zeros((chunks, CHUNK, shard_rows, width), BF16)
    last_tick = chunks + sections - 2
    for tick in range(last_tick + 1):
        outs = block_call(
            tick, sections, patch_rows, plan, norm_gain, qk_gain[0], w_project, kv_state, kept,
            before=(gathered, x_before, w_before) if tick > 0 else (),
            first=(entering,) if tick < chunks else (),
            entry=(max(0, tick - 1) * CHUNK) if tick < chunks else None,
            last=(w_out[0],) if tick == last_tick else (),
        )
        x, mixture, kv_state, kept = outs[:4]
        if tick < last_tick:
            arrived = onward(mixture)
            arrived, x = lax.optimization_barrier((arrived, x))
            x_before = onward(x)
            gathered = spread(arrived)
        if tick == 0:
            rest, gathered = lax.optimization_barrier((ordered[CHUNK:], gathered))
            entering = spread(rest)

    terms = lax.all_to_all(outs[4], "sp", 0, 0)
    own = lax.dynamic_index_in_dim(
        x.reshape(CHUNK, groups, shard_rows, width), group_no, 1, keepdims=False
    )
    results = onward(kept, -1)
    section_out = close_call(sections, patch_rows, plan, terms, own, results, latents.shape)
    return section_out[None], kv_state[None]


def solution(mesh):
    in_specs = (
        P("prompt", "sp", None),
        P("prompt"),
        P("section", None),
        P("section", None, None, "sp"),
        P("section", None, None),
        P("section", "sp", None),
        P("section", None, "prompt", "sp"),
    )
    out_specs = (P("section", "prompt", "sp", None), P("section", None, "prompt", "sp"))
    return jax.shard_map(
        on_device, mesh=mesh, in_specs=in_specs, out_specs=out_specs, check_vma=False
    )
```

```python
import math

import jax
import jax.numpy as jnp
from jax import lax
from jax.experimental import pallas as pl
from jax.experimental.pallas import tpu as pltpu
from jax.sharding import PartitionSpec as P

EPS = 1e-06
CHUNK = 2
OUT_BLOCK = 512
MIB = 1024 * 1024
BF16, F32 = jnp.bfloat16, jnp.float32
VMEM = pl.BlockSpec(memory_space=pltpu.VMEM)
SMEM = pl.BlockSpec(memory_space=pltpu.SMEM)


def onward(value, steps=1):
    count = lax.axis_size("section")
    return lax.ppermute(value, "section", [(i, (i + steps) % count) for i in range(count)])


def spread(value):
    count = lax.axis_size("sp")
    copies = jnp.broadcast_to(value[None], (count,) + value.shape)
    return lax.all_to_all(copies, "sp", 0, 0)


def blocks_of(width):
    return [slice(i, i + OUT_BLOCK) for i in range(0, width, OUT_BLOCK)]


def pick_kernel(sections, patch_rows, plan, latents, picked):
    patches = latents.shape[0]
    chunk = jnp.where(plan[patches] == 0, 0, sections - plan[patches])
    turn = jnp.minimum(chunk * CHUNK, patches - CHUNK)
    for i in range(CHUNK):
        picked[i] = latents[plan[turn + i] // patch_rows]


def pick_call(sections, patch_rows, plan, latents):
    return pl.pallas_call(
        lambda *refs: pick_kernel(sections, patch_rows, *refs),
        out_shape=jax.ShapeDtypeStruct((CHUNK,) + latents.shape[1:], latents.dtype),
        in_specs=[SMEM, VMEM],
        out_specs=VMEM,
        compiler_params=pltpu.CompilerParams(vmem_limit_bytes=4 * MIB),
    )(plan, latents)


def project_kernel(gathered, w_before, attended, mixed):
    local_width = gathered.shape[2]
    for i in range(gathered.shape[0]):
        mixed[:, i * local_width : (i + 1) * local_width] = gathered[i]
    for cols in blocks_of(attended.shape[1]):
        attended[:, cols] = jnp.dot(mixed[...], w_before[:, cols], preferred_element_type=F32)


def project_call(gathered, w_before):
    rows = gathered.shape[1]
    full, width = w_before.shape
    return pl.pallas_call(
        project_kernel,
        out_shape=jax.ShapeDtypeStruct((rows, width), F32),
        in_specs=[VMEM, VMEM],
        out_specs=VMEM,
        scratch_shapes=[pltpu.VMEM((rows, full), BF16)],
        compiler_params=pltpu.CompilerParams(vmem_limit_bytes=6 * MIB),
        cost_estimate=pl.CostEstimate(
            flops=2 * rows * full * width, bytes_accessed=2 * full * width, transcendentals=0
        ),
    )(gathered, w_before)


def block_kernel(tick, sections, patch_rows, shard_rows, finishes, *refs):
    refs = list(refs)
    plan, gain, qk_gain, w_project, kv_in = refs[:5]
    del refs[:5]
    if tick == 0:
        first = refs.pop(0)
    else:
        x_before, attended = refs[:2]
        del refs[:2]
    if tick > 1:
        kept_in = refs.pop(0)
    if finishes:
        w_last = refs.pop(0)
    x_out, mixture_out, kv_out = refs[:3]
    del refs[:3]
    if tick > 0:
        kept_out = refs.pop(0)
    if finishes:
        terms_out = refs.pop(0)
    normed, x_wide = refs
    rows, width = x_out.shape
    local_width = kv_out.shape[2]
    head_dim = qk_gain.shape[1]
    patches = plan.shape[0] - 2
    chunks = patches // CHUNK
    section_no, group_no = plan[patches], plan[patches + 1]
    blocks = blocks_of(width)

    kv_out[...] = kv_in[...]
    squares = jnp.zeros((rows, 1), F32)
    if tick == 0:
        for i in range(CHUNK):
            for g in range(first.shape[0]):
                at = i * patch_rows + g * shard_rows
                x_wide[at : at + shard_rows, :] = first[g, i].astype(F32)
    else:
        slot_kept = tick - jnp.where(section_no == 0, sections, section_no)
        if tick > 1:
            kept_out[...] = kept_in[...]
        else:
            kept_out[...] = jnp.zeros(kept_out.shape, BF16)
    for cols in blocks:
        if tick == 0:
            x = x_wide[:, cols]
        else:
            x = x_before[:, cols].astype(F32)
            x = jnp.where(slot_kept >= 0, x + attended[:, cols], x).astype(BF16).astype(F32)
            x_wide[:, cols] = x
        squares += jnp.sum(x * x, axis=-1, keepdims=True)
        x_out[:, cols] = x.astype(BF16)
    scale = lax.rsqrt(squares / width + EPS)
    for cols in blocks:
        normed[:, cols] = (x_wide[:, cols] * scale * gain[:, cols]).astype(BF16)

    def keep():
        for i in range(CHUNK):
            at = pl.multiple_of(i * patch_rows + group_no * shard_rows, shard_rows)
            kept_out[slot_kept, i] = x_wide[pl.ds(at, shard_rows), :].astype(BF16)

    def projected(i):
        return jnp.dot(normed[...], w_project[i], preferred_element_type=F32)

    def head_norm(values, gains):
        parts = []
        for h in range(local_width // head_dim):
            part = values[:, h * head_dim : (h + 1) * head_dim]
            part = part * lax.rsqrt(jnp.mean(part * part, axis=-1, keepdims=True) + EPS)
            parts.append((part * gains).astype(BF16))
        return parts

    queries = head_norm(projected(0), qk_gain[0:1, :])
    keys_new = jnp.concatenate(head_norm(projected(1), qk_gain[1:2, :]), axis=1)
    values_new = projected(2).astype(BF16)
    slot = tick - section_no
    active = (slot >= 0) & (slot < chunks)
    turn = jnp.clip(slot, 0, chunks - 1) * CHUNK
    places = [
        pl.ds(pl.multiple_of(plan[turn + i], patch_rows), patch_rows) for i in range(CHUNK)
    ]
    stale = [kv_in[i, places[1], :] for i in range(2)]
    for i in range(CHUNK):
        part = slice(i * patch_rows, (i + 1) * patch_rows)
        kv_out[0, places[i], :] = jnp.where(active, keys_new[part], kv_in[0, places[i], :])
        kv_out[1, places[i], :] = jnp.where(active, values_new[part], kv_in[1, places[i], :])
    token = lax.broadcasted_iota(jnp.int32, (rows, kv_out.shape[1]), 1) - plan[turn + 1]
    row = lax.broadcasted_iota(jnp.int32, (rows, kv_out.shape[1]), 0)
    hidden = (row < patch_rows) & (token >= 0) & (token < patch_rows)
    contract = (((1,), (1,)), ((), ()))
    shrink = 1.0 / math.sqrt(head_dim)
    for h in range(local_width // head_dim):
        cols = slice(h * head_dim, (h + 1) * head_dim)
        scores = lax.dot_general(
            queries[h], kv_out[0, :, cols], contract, preferred_element_type=F32
        )
        scores = jnp.where(hidden, -jnp.inf, scores * shrink)
        older = lax.dot_general(
            queries[h], stale[0][:, cols], contract, preferred_element_type=F32
        )
        is_first = lax.broadcasted_iota(jnp.int32, older.shape, 0) < patch_rows
        older = jnp.where(is_first, older * shrink, -jnp.inf)
        peak = jnp.maximum(
            jnp.max(scores, axis=-1, keepdims=True), jnp.max(older, axis=-1, keepdims=True)
        )
        weights, older = jnp.exp(scores - peak), jnp.exp(older - peak)
        share = 1.0 / (
            jnp.sum(weights, axis=-1, keepdims=True) + jnp.sum(older, axis=-1, keepdims=True)
        )
        mixture = jnp.dot(
            (weights * share).astype(BF16), kv_out[1, :, cols], preferred_element_type=F32
        )
        mixture += jnp.dot(
            (older * share).astype(BF16), stale[1][:, cols], preferred_element_type=F32
        )
        mixture_out[:, cols] = mixture.astype(BF16)
    if tick > 0:
        pl.when((slot_kept >= 0) & (slot_kept < chunks))(keep)
    if finishes:
        for cols in blocks:
            terms = jnp.dot(mixture_out[...], w_last[:, cols], preferred_element_type=F32)
            for i in range(CHUNK):
                for g in range(terms_out.shape[0]):
                    at = i * patch_rows + g * shard_rows
                    terms_out[g, i, :, cols] = terms[at : at + shard_rows].astype(BF16)


def block_call(tick, sections, patch_rows, shard_rows, plan, gain, qk_gain, w_project, kv_state,
               inputs, kept=(), last=()):
    width = gain.shape[1]
    local_width = kv_state.shape[2]
    rows = CHUNK * patch_rows
    macs = rows * width * local_width * 3
    out_shape = [
        jax.ShapeDtypeStruct((rows, width), BF16),
        jax.ShapeDtypeStruct((rows, local_width), BF16),
        jax.ShapeDtypeStruct(kv_state.shape, kv_state.dtype),
    ]
    chunks = (plan.shape[0] - 2) // CHUNK
    if tick > 0:
        out_shape.append(jax.ShapeDtypeStruct((chunks, CHUNK, shard_rows, width), BF16))
    if last:
        groups = patch_rows // shard_rows
        out_shape.append(jax.ShapeDtypeStruct((groups, CHUNK, shard_rows, width), BF16))
    operands = (gain, qk_gain, w_project, kv_state, *inputs, *kept, *last)
    return pl.pallas_call(
        lambda *refs: block_kernel(tick, sections, patch_rows, shard_rows, bool(last), *refs),
        out_shape=out_shape,
        in_specs=[SMEM] + [VMEM] * len(operands),
        out_specs=[VMEM] * len(out_shape),
        scratch_shapes=[pltpu.VMEM((rows, width), BF16), pltpu.VMEM((rows, width), F32)],
        compiler_params=pltpu.CompilerParams(vmem_limit_bytes=10 * MIB),
        cost_estimate=pl.CostEstimate(
            flops=2 * macs, bytes_accessed=2 * macs // rows, transcendentals=0
        ),
    )(plan, *operands)


def close_kernel(sections, patch_rows, plan, terms, own, results, section_out):
    patches = section_out.shape[0]
    section_no = plan[patches]
    for j in range(patches):
        section_out[plan[j] // patch_rows] = results[j // CHUNK, j % CHUNK]

    @pl.when(section_no == sections - 1)
    def _():
        for i in range(CHUNK):
            total = own[i].astype(F32)
            for g in range(terms.shape[0]):
                total += terms[g, i].astype(F32)
            section_out[plan[patches - CHUNK + i] // patch_rows] = total.astype(BF16)


def close_call(sections, patch_rows, plan, terms, own, results, shape):
    return pl.pallas_call(
        lambda *refs: close_kernel(sections, patch_rows, *refs),
        out_shape=jax.ShapeDtypeStruct(shape, BF16),
        in_specs=[SMEM, VMEM, VMEM, VMEM],
        out_specs=VMEM,
        compiler_params=pltpu.CompilerParams(vmem_limit_bytes=6 * MIB),
    )(plan, terms, own, results)


def on_device(latents, offsets, norm_gain, w_qkv, qk_gain, w_out, kv_cache):
    groups = lax.axis_size("sp")
    sections = lax.axis_size("section")
    section_no = lax.axis_index("section")
    group_no = lax.axis_index("sp")
    prompt_no = lax.axis_index("prompt")
    prompts = lax.axis_size("prompt")
    patches, shard_rows, width = latents.shape
    patch_rows = shard_rows * groups
    local_width = w_out.shape[1]
    chunks = patches // CHUNK
    plan = jnp.concatenate([offsets, jnp.stack([section_no, group_no]).astype(jnp.int32)])

    share = local_width // prompts
    own_share = lax.dynamic_slice_in_dim(w_out[0], prompt_no * share, share, 0)
    own_share, latents = lax.optimization_barrier((own_share, latents))
    moved = onward(own_share)
    entering = spread(pick_call(sections, patch_rows, plan, latents))
    w_before = lax.all_gather(moved, ("sp", "prompt"), axis=0, tiled=True)
    w_project = jnp.swapaxes(w_qkv[0], 0, 1)

    kv_state = kv_cache[0]
    last_tick = chunks + sections - 2
    for tick in range(last_tick + 1):
        if tick == 0:
            inputs = (entering,)
        else:
            inputs = (x_before, project_call(gathered, w_before))
        outs = block_call(
            tick, sections, patch_rows, shard_rows, plan, norm_gain, qk_gain[0], w_project,
            kv_state, inputs, kept=(kept,) if tick > 1 else (),
            last=(w_out[0],) if tick == last_tick else (),
        )
        x, mixture, kv_state = outs[:3]
        if tick > 0:
            kept = outs[3]
        if tick < last_tick:
            arrived = onward(mixture)
            arrived, x = lax.optimization_barrier((arrived, x))
            x_before = onward(x)
            gathered = spread(arrived)

    terms = lax.all_to_all(outs[-1], "sp", 0, 0)
    own = x.reshape(CHUNK, groups, shard_rows, width)
    own = lax.dynamic_index_in_dim(own, group_no, 1, keepdims=False)
    results = onward(kept, -1)
    section_out = close_call(sections, patch_rows, plan, terms, own, results, latents.shape)
    return section_out[None], kv_state[None]


def solution(mesh):
    in_specs = (
        P("prompt", "sp", None),
        P("prompt"),
        P("section", None),
        P("section", None, None, "sp"),
        P("section", None, None),
        P("section", "sp", None),
        P("section", None, "prompt", "sp"),
    )
    out_specs = (P("section", "prompt", "sp", None), P("section", None, "prompt", "sp"))
    return jax.shard_map(
        on_device, mesh=mesh, in_specs=in_specs, out_specs=out_specs, check_vma=False
    )
```

```python
import math

import jax
import jax.numpy as jnp
from jax import lax
from jax.experimental import pallas as pl
from jax.experimental.pallas import tpu as pltpu
from jax.sharding import PartitionSpec as P

EPS = 1e-06
CHUNK = 2
OUT_BLOCK = 512
MIB = 1024 * 1024
BF16, F32 = jnp.bfloat16, jnp.float32
VMEM = pl.BlockSpec(memory_space=pltpu.VMEM)
SMEM = pl.BlockSpec(memory_space=pltpu.SMEM)


def onward(value, steps=1):
    count = lax.axis_size("section")
    return lax.ppermute(value, "section", [(i, (i + steps) % count) for i in range(count)])


def spread(value):
    count = lax.axis_size("sp")
    copies = jnp.broadcast_to(value[None], (count,) + value.shape)
    return lax.all_to_all(copies, "sp", 0, 0)


def blocks_of(width):
    return [slice(i, i + OUT_BLOCK) for i in range(0, width, OUT_BLOCK)]


def pick_kernel(sections, patch_rows, plan, latents, picked):
    patches = latents.shape[0]
    chunk = jnp.where(plan[patches] == 0, 0, sections - plan[patches])
    turn = jnp.minimum(chunk * CHUNK, patches - CHUNK)
    for i in range(CHUNK):
        picked[i] = latents[plan[turn + i] // patch_rows]


def pick_call(sections, patch_rows, plan, latents):
    return pl.pallas_call(
        lambda *refs: pick_kernel(sections, patch_rows, *refs),
        out_shape=jax.ShapeDtypeStruct((CHUNK,) + latents.shape[1:], latents.dtype),
        in_specs=[SMEM, VMEM],
        out_specs=VMEM,
        compiler_params=pltpu.CompilerParams(vmem_limit_bytes=4 * MIB),
    )(plan, latents)


def project_kernel(gathered, w_before, attended, mixed):
    local_width = gathered.shape[2]
    for i in range(gathered.shape[0]):
        mixed[:, i * local_width : (i + 1) * local_width] = gathered[i]
    for cols in blocks_of(attended.shape[1]):
        attended[:, cols] = jnp.dot(mixed[...], w_before[:, cols], preferred_element_type=F32)


def project_call(gathered, w_before):
    rows = gathered.shape[1]
    full, width = w_before.shape
    return pl.pallas_call(
        project_kernel,
        out_shape=jax.ShapeDtypeStruct((rows, width), F32),
        in_specs=[VMEM, VMEM],
        out_specs=VMEM,
        scratch_shapes=[pltpu.VMEM((rows, full), BF16)],
        compiler_params=pltpu.CompilerParams(vmem_limit_bytes=6 * MIB),
        cost_estimate=pl.CostEstimate(
            flops=4 * rows * full * width, bytes_accessed=2 * full * width, transcendentals=0
        ),
    )(gathered, w_before)


def block_kernel(tick, sections, patch_rows, shard_rows, finishes, *refs):
    refs = list(refs)
    plan, gain, qk_gain, w_project, kv_in = refs[:5]
    del refs[:5]
    if tick == 0:
        first = refs.pop(0)
    else:
        x_before, attended = refs[:2]
        del refs[:2]
    if tick > 1:
        kept_in = refs.pop(0)
    if finishes:
        w_last = refs.pop(0)
    x_out, mixture_out, kv_out = refs[:3]
    del refs[:3]
    if tick > 0:
        kept_out = refs.pop(0)
    if finishes:
        terms_out = refs.pop(0)
    normed, x_wide = refs
    rows, width = x_out.shape
    local_width = kv_out.shape[2]
    head_dim = qk_gain.shape[1]
    patches = plan.shape[0] - 2
    chunks = patches // CHUNK
    section_no, group_no = plan[patches], plan[patches + 1]
    blocks = blocks_of(width)

    kv_out[...] = kv_in[...]
    squares = jnp.zeros((rows, 1), F32)
    if tick == 0:
        for i in range(CHUNK):
            for g in range(first.shape[0]):
                at = i * patch_rows + g * shard_rows
                x_wide[at : at + shard_rows, :] = first[g, i].astype(F32)
    else:
        slot_kept = tick - jnp.where(section_no == 0, sections, section_no)
        if tick > 1:
            kept_out[...] = kept_in[...]
        else:
            kept_out[...] = jnp.zeros(kept_out.shape, BF16)
    for cols in blocks:
        if tick == 0:
            x = x_wide[:, cols]
        else:
            x = x_before[:, cols].astype(F32)
            x = jnp.where(slot_kept >= 0, x + attended[:, cols], x).astype(BF16).astype(F32)
            x_wide[:, cols] = x
        squares += jnp.sum(x * x, axis=-1, keepdims=True)
        x_out[:, cols] = x.astype(BF16)
    scale = lax.rsqrt(squares / width + EPS)
    for cols in blocks:
        normed[:, cols] = (x_wide[:, cols] * scale * gain[:, cols]).astype(BF16)

    def keep():
        for i in range(CHUNK):
            at = pl.multiple_of(i * patch_rows + group_no * shard_rows, shard_rows)
            kept_out[slot_kept, i] = x_wide[pl.ds(at, shard_rows), :].astype(BF16)

    def projected(i):
        return jnp.dot(normed[...], w_project[i], preferred_element_type=F32)

    def head_norm(values, gains):
        parts = []
        for h in range(local_width // head_dim):
            part = values[:, h * head_dim : (h + 1) * head_dim]
            part = part * lax.rsqrt(jnp.mean(part * part, axis=-1, keepdims=True) + EPS)
            parts.append((part * gains).astype(BF16))
        return parts

    queries = head_norm(projected(0), qk_gain[0:1, :])
    keys_new = jnp.concatenate(head_norm(projected(1), qk_gain[1:2, :]), axis=1)
    values_new = projected(2).astype(BF16)
    slot = tick - section_no
    active = (slot >= 0) & (slot < chunks)
    turn = jnp.clip(slot, 0, chunks - 1) * CHUNK
    places = [
        pl.ds(pl.multiple_of(plan[turn + i], patch_rows), patch_rows) for i in range(CHUNK)
    ]
    stale = [kv_in[i, places[1], :] for i in range(2)]
    for i in range(CHUNK):
        part = slice(i * patch_rows, (i + 1) * patch_rows)
        kv_out[0, places[i], :] = jnp.where(active, keys_new[part], kv_in[0, places[i], :])
        kv_out[1, places[i], :] = jnp.where(active, values_new[part], kv_in[1, places[i], :])
    token = lax.broadcasted_iota(jnp.int32, (rows, kv_out.shape[1]), 1) - plan[turn + 1]
    row = lax.broadcasted_iota(jnp.int32, (rows, kv_out.shape[1]), 0)
    hidden = (row < patch_rows) & (token >= 0) & (token < patch_rows)
    contract = (((1,), (1,)), ((), ()))
    shrink = 1.0 / math.sqrt(head_dim)
    for h in range(local_width // head_dim):
        cols = slice(h * head_dim, (h + 1) * head_dim)
        scores = lax.dot_general(
            queries[h], kv_out[0, :, cols], contract, preferred_element_type=F32
        )
        scores = jnp.where(hidden, -jnp.inf, scores * shrink)
        older = lax.dot_general(
            queries[h], stale[0][:, cols], contract, preferred_element_type=F32
        )
        is_first = lax.broadcasted_iota(jnp.int32, older.shape, 0) < patch_rows
        older = jnp.where(is_first, older * shrink, -jnp.inf)
        peak = jnp.maximum(
            jnp.max(scores, axis=-1, keepdims=True), jnp.max(older, axis=-1, keepdims=True)
        )
        weights, older = jnp.exp(scores - peak), jnp.exp(older - peak)
        share = 1.0 / (
            jnp.sum(weights, axis=-1, keepdims=True) + jnp.sum(older, axis=-1, keepdims=True)
        )
        mixture = jnp.dot(
            (weights * share).astype(BF16), kv_out[1, :, cols], preferred_element_type=F32
        )
        mixture += jnp.dot(
            (older * share).astype(BF16), stale[1][:, cols], preferred_element_type=F32
        )
        mixture_out[:, cols] = mixture.astype(BF16)
    if tick > 0:
        pl.when((slot_kept >= 0) & (slot_kept < chunks))(keep)
    if finishes:
        for cols in blocks:
            terms = jnp.dot(mixture_out[...], w_last[:, cols], preferred_element_type=F32)
            for i in range(CHUNK):
                for g in range(terms_out.shape[0]):
                    at = i * patch_rows + g * shard_rows
                    terms_out[g, i, :, cols] = terms[at : at + shard_rows].astype(BF16)


def block_call(tick, sections, patch_rows, shard_rows, plan, gain, qk_gain, w_project, kv_state,
               inputs, kept=(), last=()):
    width = gain.shape[1]
    local_width = kv_state.shape[2]
    rows = CHUNK * patch_rows
    macs = rows * width * local_width * 3
    out_shape = [
        jax.ShapeDtypeStruct((rows, width), BF16),
        jax.ShapeDtypeStruct((rows, local_width), BF16),
        jax.ShapeDtypeStruct(kv_state.shape, kv_state.dtype),
    ]
    chunks = (plan.shape[0] - 2) // CHUNK
    if tick > 0:
        out_shape.append(jax.ShapeDtypeStruct((chunks, CHUNK, shard_rows, width), BF16))
    if last:
        groups = patch_rows // shard_rows
        out_shape.append(jax.ShapeDtypeStruct((groups, CHUNK, shard_rows, width), BF16))
    operands = (gain, qk_gain, w_project, kv_state, *inputs, *kept, *last)
    return pl.pallas_call(
        lambda *refs: block_kernel(tick, sections, patch_rows, shard_rows, bool(last), *refs),
        out_shape=out_shape,
        in_specs=[SMEM] + [VMEM] * len(operands),
        out_specs=[VMEM] * len(out_shape),
        scratch_shapes=[pltpu.VMEM((rows, width), BF16), pltpu.VMEM((rows, width), F32)],
        compiler_params=pltpu.CompilerParams(vmem_limit_bytes=10 * MIB),
        cost_estimate=pl.CostEstimate(
            flops=2 * macs, bytes_accessed=2 * macs // rows, transcendentals=0
        ),
    )(plan, *operands)


def close_kernel(sections, patch_rows, plan, terms, own, results, section_out):
    patches = section_out.shape[0]
    section_no = plan[patches]
    for j in range(patches):
        section_out[plan[j] // patch_rows] = results[j // CHUNK, j % CHUNK]

    @pl.when(section_no == sections - 1)
    def _():
        for i in range(CHUNK):
            total = own[i].astype(F32)
            for g in range(terms.shape[0]):
                total += terms[g, i].astype(F32)
            section_out[plan[patches - CHUNK + i] // patch_rows] = total.astype(BF16)


def close_call(sections, patch_rows, plan, terms, own, results, shape):
    return pl.pallas_call(
        lambda *refs: close_kernel(sections, patch_rows, *refs),
        out_shape=jax.ShapeDtypeStruct(shape, BF16),
        in_specs=[SMEM, VMEM, VMEM, VMEM],
        out_specs=VMEM,
        compiler_params=pltpu.CompilerParams(vmem_limit_bytes=6 * MIB),
    )(plan, terms, own, results)


def on_device(latents, offsets, norm_gain, w_qkv, qk_gain, w_out, kv_cache):
    groups = lax.axis_size("sp")
    sections = lax.axis_size("section")
    section_no = lax.axis_index("section")
    group_no = lax.axis_index("sp")
    prompt_no = lax.axis_index("prompt")
    prompts = lax.axis_size("prompt")
    patches, shard_rows, width = latents.shape
    patch_rows = shard_rows * groups
    local_width = w_out.shape[1]
    chunks = patches // CHUNK
    plan = jnp.concatenate([offsets, jnp.stack([section_no, group_no]).astype(jnp.int32)])

    share = local_width // prompts
    own_share = lax.dynamic_slice_in_dim(w_out[0], prompt_no * share, share, 0)
    own_share, latents = lax.optimization_barrier((own_share, latents))
    moved = onward(own_share)
    entering = spread(pick_call(sections, patch_rows, plan, latents))
    w_before = lax.all_gather(moved, ("sp", "prompt"), axis=0, tiled=True)
    w_project = jnp.swapaxes(w_qkv[0], 0, 1)

    kv_state = kv_cache[0]
    last_tick = chunks + sections - 2
    for tick in range(last_tick + 1):
        if tick == 0:
            inputs = (entering,)
        else:
            inputs = (x_before, project_call(gathered, w_before))
        outs = block_call(
            tick, sections, patch_rows, shard_rows, plan, norm_gain, qk_gain[0], w_project,
            kv_state, inputs, kept=(kept,) if tick > 1 else (),
            last=(w_out[0],) if tick == last_tick else (),
        )
        x, mixture, kv_state = outs[:3]
        if tick > 0:
            kept = outs[3]
        if tick < last_tick:
            x_before = onward(x)
            arrived = onward(mixture)
            gathered = spread(arrived)

    terms = lax.all_to_all(outs[-1], "sp", 0, 0)
    own = x.reshape(CHUNK, groups, shard_rows, width)
    own = lax.dynamic_index_in_dim(own, group_no, 1, keepdims=False)
    results = onward(kept, -1)
    section_out = close_call(sections, patch_rows, plan, terms, own, results, latents.shape)
    return section_out[None], kv_state[None]


def solution(mesh):
    in_specs = (
        P("prompt", "sp", None),
        P("prompt"),
        P("section", None),
        P("section", None, None, "sp"),
        P("section", None, None),
        P("section", "sp", None),
        P("section", None, "prompt", "sp"),
    )
    out_specs = (P("section", "prompt", "sp", None), P("section", None, "prompt", "sp"))
    return jax.shard_map(
        on_device, mesh=mesh, in_specs=in_specs, out_specs=out_specs, check_vma=False
    )
```

```python
import math

import jax
import jax.numpy as jnp
from jax import lax
from jax.experimental import pallas as pl
from jax.experimental.pallas import tpu as pltpu
from jax.sharding import PartitionSpec as P

EPS = 1e-06
CHUNK = 2
OUT_BLOCK = 512
MIB = 1024 * 1024
BF16, F32 = jnp.bfloat16, jnp.float32
VMEM = pl.BlockSpec(memory_space=pltpu.VMEM)
SMEM = pl.BlockSpec(memory_space=pltpu.SMEM)


def onward(value, steps=1):
    count = lax.axis_size("section")
    return lax.ppermute(value, "section", [(i, (i + steps) % count) for i in range(count)])


def spread(value):
    count = lax.axis_size("sp")
    copies = jnp.broadcast_to(value[None], (count,) + value.shape)
    return lax.all_to_all(copies, "sp", 0, 0)


def blocks_of(width):
    return [slice(i, i + OUT_BLOCK) for i in range(0, width, OUT_BLOCK)]


def pick_kernel(sections, patch_rows, plan, latents, picked):
    patches = latents.shape[0]
    chunk = jnp.where(plan[patches] == 0, 0, sections - plan[patches])
    turn = jnp.minimum(chunk * CHUNK, patches - CHUNK)
    for i in range(CHUNK):
        picked[i] = latents[plan[turn + i] // patch_rows]


def pick_call(sections, patch_rows, plan, latents):
    return pl.pallas_call(
        lambda *refs: pick_kernel(sections, patch_rows, *refs),
        out_shape=jax.ShapeDtypeStruct((CHUNK,) + latents.shape[1:], latents.dtype),
        in_specs=[SMEM, VMEM],
        out_specs=VMEM,
        compiler_params=pltpu.CompilerParams(vmem_limit_bytes=4 * MIB),
    )(plan, latents)


def project_kernel(gathered, w_before, attended, mixed):
    local_width = gathered.shape[2]
    for i in range(gathered.shape[0]):
        mixed[:, i * local_width : (i + 1) * local_width] = gathered[i]
    for cols in blocks_of(attended.shape[1]):
        attended[:, cols] = jnp.dot(mixed[...], w_before[:, cols], preferred_element_type=F32)


def stream_kernel(gathered, w_before, attended, mixed, w_here, sems):
    local_width = gathered.shape[2]
    blocks = blocks_of(attended.shape[1])
    copies = []
    for i, cols in enumerate(blocks):
        span = pl.ds(cols.start, OUT_BLOCK)
        copies.append(pltpu.make_async_copy(w_before.at[:, span], w_here.at[:, span], sems.at[i]))
        copies[i].start()
    for i in range(gathered.shape[0]):
        mixed[:, i * local_width : (i + 1) * local_width] = gathered[i]
    for i, cols in enumerate(blocks):
        copies[i].wait()
        attended[:, cols] = jnp.dot(mixed[...], w_here[:, cols], preferred_element_type=F32)


def stream_call(gathered, w_before):
    rows = gathered.shape[1]
    full, width = w_before.shape
    return pl.pallas_call(
        stream_kernel,
        out_shape=jax.ShapeDtypeStruct((rows, width), F32),
        in_specs=[VMEM, pl.BlockSpec(memory_space=pl.ANY)],
        out_specs=VMEM,
        scratch_shapes=[
            pltpu.VMEM((rows, full), BF16),
            pltpu.VMEM((full, width), BF16),
            pltpu.SemaphoreType.DMA((width // OUT_BLOCK,)),
        ],
        compiler_params=pltpu.CompilerParams(vmem_limit_bytes=44 * MIB),
        cost_estimate=pl.CostEstimate(
            flops=4 * rows * full * width, bytes_accessed=2 * full * width, transcendentals=0
        ),
    )(gathered, w_before)


def project_call(gathered, w_before):
    rows = gathered.shape[1]
    full, width = w_before.shape
    return pl.pallas_call(
        project_kernel,
        out_shape=jax.ShapeDtypeStruct((rows, width), F32),
        in_specs=[VMEM, VMEM],
        out_specs=VMEM,
        scratch_shapes=[pltpu.VMEM((rows, full), BF16)],
        compiler_params=pltpu.CompilerParams(vmem_limit_bytes=6 * MIB),
        cost_estimate=pl.CostEstimate(
            flops=4 * rows * full * width, bytes_accessed=2 * full * width, transcendentals=0
        ),
    )(gathered, w_before)


def block_kernel(tick, sections, patch_rows, shard_rows, finishes, *refs):
    refs = list(refs)
    plan, gain, qk_gain, w_project, kv_in = refs[:5]
    del refs[:5]
    if tick == 0:
        first = refs.pop(0)
    else:
        x_before, attended = refs[:2]
        del refs[:2]
    if tick > 1:
        kept_in = refs.pop(0)
    if finishes:
        w_last = refs.pop(0)
    x_out, mixture_out, kv_out = refs[:3]
    del refs[:3]
    if tick > 0:
        kept_out = refs.pop(0)
    if finishes:
        terms_out = refs.pop(0)
    normed, x_wide = refs
    rows, width = x_out.shape
    local_width = kv_out.shape[2]
    head_dim = qk_gain.shape[1]
    patches = plan.shape[0] - 2
    chunks = patches // CHUNK
    section_no, group_no = plan[patches], plan[patches + 1]
    blocks = blocks_of(width)

    kv_out[...] = kv_in[...]
    squares = jnp.zeros((rows, 1), F32)
    if tick == 0:
        for i in range(CHUNK):
            for g in range(first.shape[0]):
                at = i * patch_rows + g * shard_rows
                x_wide[at : at + shard_rows, :] = first[g, i].astype(F32)
    else:
        slot_kept = tick - jnp.where(section_no == 0, sections, section_no)
        if tick > 1:
            kept_out[...] = kept_in[...]
        else:
            kept_out[...] = jnp.zeros(kept_out.shape, BF16)
    for cols in blocks:
        if tick == 0:
            x = x_wide[:, cols]
        else:
            x = x_before[:, cols].astype(F32)
            x = jnp.where(slot_kept >= 0, x + attended[:, cols], x).astype(BF16).astype(F32)
            x_wide[:, cols] = x
        squares += jnp.sum(x * x, axis=-1, keepdims=True)
        x_out[:, cols] = x.astype(BF16)
    scale = lax.rsqrt(squares / width + EPS)
    for cols in blocks:
        normed[:, cols] = (x_wide[:, cols] * scale * gain[:, cols]).astype(BF16)

    def keep():
        for i in range(CHUNK):
            at = pl.multiple_of(i * patch_rows + group_no * shard_rows, shard_rows)
            kept_out[slot_kept, i] = x_wide[pl.ds(at, shard_rows), :].astype(BF16)

    def projected(i):
        return jnp.dot(normed[...], w_project[i], preferred_element_type=F32)

    def head_norm(values, gains):
        parts = []
        for h in range(local_width // head_dim):
            part = values[:, h * head_dim : (h + 1) * head_dim]
            part = part * lax.rsqrt(jnp.mean(part * part, axis=-1, keepdims=True) + EPS)
            parts.append((part * gains).astype(BF16))
        return parts

    queries = head_norm(projected(0), qk_gain[0:1, :])
    keys_new = jnp.concatenate(head_norm(projected(1), qk_gain[1:2, :]), axis=1)
    values_new = projected(2).astype(BF16)
    slot = tick - section_no
    active = (slot >= 0) & (slot < chunks)
    turn = jnp.clip(slot, 0, chunks - 1) * CHUNK
    places = [
        pl.ds(pl.multiple_of(plan[turn + i], patch_rows), patch_rows) for i in range(CHUNK)
    ]
    stale = [kv_in[i, places[1], :] for i in range(2)]
    for i in range(CHUNK):
        part = slice(i * patch_rows, (i + 1) * patch_rows)
        kv_out[0, places[i], :] = jnp.where(active, keys_new[part], kv_in[0, places[i], :])
        kv_out[1, places[i], :] = jnp.where(active, values_new[part], kv_in[1, places[i], :])
    token = lax.broadcasted_iota(jnp.int32, (rows, kv_out.shape[1]), 1) - plan[turn + 1]
    row = lax.broadcasted_iota(jnp.int32, (rows, kv_out.shape[1]), 0)
    hidden = (row < patch_rows) & (token >= 0) & (token < patch_rows)
    contract = (((1,), (1,)), ((), ()))
    shrink = 1.0 / math.sqrt(head_dim)
    for h in range(local_width // head_dim):
        cols = slice(h * head_dim, (h + 1) * head_dim)
        scores = lax.dot_general(
            queries[h], kv_out[0, :, cols], contract, preferred_element_type=F32
        )
        scores = jnp.where(hidden, -jnp.inf, scores * shrink)
        older = lax.dot_general(
            queries[h], stale[0][:, cols], contract, preferred_element_type=F32
        )
        is_first = lax.broadcasted_iota(jnp.int32, older.shape, 0) < patch_rows
        older = jnp.where(is_first, older * shrink, -jnp.inf)
        peak = jnp.maximum(
            jnp.max(scores, axis=-1, keepdims=True), jnp.max(older, axis=-1, keepdims=True)
        )
        weights, older = jnp.exp(scores - peak), jnp.exp(older - peak)
        share = 1.0 / (
            jnp.sum(weights, axis=-1, keepdims=True) + jnp.sum(older, axis=-1, keepdims=True)
        )
        mixture = jnp.dot(
            (weights * share).astype(BF16), kv_out[1, :, cols], preferred_element_type=F32
        )
        mixture += jnp.dot(
            (older * share).astype(BF16), stale[1][:, cols], preferred_element_type=F32
        )
        mixture_out[:, cols] = mixture.astype(BF16)
    if tick > 0:
        pl.when((slot_kept >= 0) & (slot_kept < chunks))(keep)
    if finishes:
        for cols in blocks:
            terms = jnp.dot(mixture_out[...], w_last[:, cols], preferred_element_type=F32)
            for i in range(CHUNK):
                for g in range(terms_out.shape[0]):
                    at = i * patch_rows + g * shard_rows
                    terms_out[g, i, :, cols] = terms[at : at + shard_rows].astype(BF16)


def block_call(tick, sections, patch_rows, shard_rows, plan, gain, qk_gain, w_project, kv_state,
               inputs, kept=(), last=()):
    width = gain.shape[1]
    local_width = kv_state.shape[2]
    rows = CHUNK * patch_rows
    macs = rows * width * local_width * 3
    out_shape = [
        jax.ShapeDtypeStruct((rows, width), BF16),
        jax.ShapeDtypeStruct((rows, local_width), BF16),
        jax.ShapeDtypeStruct(kv_state.shape, kv_state.dtype),
    ]
    chunks = (plan.shape[0] - 2) // CHUNK
    if tick > 0:
        out_shape.append(jax.ShapeDtypeStruct((chunks, CHUNK, shard_rows, width), BF16))
    if last:
        groups = patch_rows // shard_rows
        out_shape.append(jax.ShapeDtypeStruct((groups, CHUNK, shard_rows, width), BF16))
    operands = (gain, qk_gain, w_project, kv_state, *inputs, *kept, *last)
    return pl.pallas_call(
        lambda *refs: block_kernel(tick, sections, patch_rows, shard_rows, bool(last), *refs),
        out_shape=out_shape,
        in_specs=[SMEM] + [VMEM] * len(operands),
        out_specs=[VMEM] * len(out_shape),
        scratch_shapes=[pltpu.VMEM((rows, width), BF16), pltpu.VMEM((rows, width), F32)],
        compiler_params=pltpu.CompilerParams(vmem_limit_bytes=10 * MIB),
        cost_estimate=pl.CostEstimate(
            flops=2 * macs, bytes_accessed=2 * macs // rows, transcendentals=0
        ),
    )(plan, *operands)


def close_kernel(sections, patch_rows, plan, terms, own, results, section_out):
    patches = section_out.shape[0]
    section_no = plan[patches]
    for j in range(patches):
        section_out[plan[j] // patch_rows] = results[j // CHUNK, j % CHUNK]

    @pl.when(section_no == sections - 1)
    def _():
        for i in range(CHUNK):
            total = own[i].astype(F32)
            for g in range(terms.shape[0]):
                total += terms[g, i].astype(F32)
            section_out[plan[patches - CHUNK + i] // patch_rows] = total.astype(BF16)


def close_call(sections, patch_rows, plan, terms, own, results, shape):
    return pl.pallas_call(
        lambda *refs: close_kernel(sections, patch_rows, *refs),
        out_shape=jax.ShapeDtypeStruct(shape, BF16),
        in_specs=[SMEM, VMEM, VMEM, VMEM],
        out_specs=VMEM,
        compiler_params=pltpu.CompilerParams(vmem_limit_bytes=6 * MIB),
    )(plan, terms, own, results)


def on_device(latents, offsets, norm_gain, w_qkv, qk_gain, w_out, kv_cache):
    groups = lax.axis_size("sp")
    sections = lax.axis_size("section")
    section_no = lax.axis_index("section")
    group_no = lax.axis_index("sp")
    prompt_no = lax.axis_index("prompt")
    prompts = lax.axis_size("prompt")
    patches, shard_rows, width = latents.shape
    patch_rows = shard_rows * groups
    local_width = w_out.shape[1]
    chunks = patches // CHUNK
    plan = jnp.concatenate([offsets, jnp.stack([section_no, group_no]).astype(jnp.int32)])

    share = local_width // prompts
    own_share = lax.dynamic_slice_in_dim(w_out[0], prompt_no * share, share, 0)
    own_share, latents = lax.optimization_barrier((own_share, latents))
    moved = onward(own_share)
    entering = spread(pick_call(sections, patch_rows, plan, latents))
    w_before = lax.all_gather(moved, ("sp", "prompt"), axis=0, tiled=True)
    w_project = jnp.swapaxes(w_qkv[0], 0, 1)

    kv_state = kv_cache[0]
    last_tick = chunks + sections - 2
    for tick in range(last_tick + 1):
        if tick == 0:
            inputs = (entering,)
        else:
            call = stream_call if tick == 1 else project_call
            inputs = (x_before, call(gathered, w_before))
        outs = block_call(
            tick, sections, patch_rows, shard_rows, plan, norm_gain, qk_gain[0], w_project,
            kv_state, inputs, kept=(kept,) if tick > 1 else (),
            last=(w_out[0],) if tick == last_tick else (),
        )
        x, mixture, kv_state = outs[:3]
        if tick > 0:
            kept = outs[3]
        if tick < last_tick:
            x_before = onward(x)
            arrived = onward(mixture)
            gathered = spread(arrived)

    terms = lax.all_to_all(outs[-1], "sp", 0, 0)
    own = x.reshape(CHUNK, groups, shard_rows, width)
    own = lax.dynamic_index_in_dim(own, group_no, 1, keepdims=False)
    results = onward(kept, -1)
    section_out = close_call(sections, patch_rows, plan, terms, own, results, latents.shape)
    return section_out[None], kv_state[None]


def solution(mesh):
    in_specs = (
        P("prompt", "sp", None),
        P("prompt"),
        P("section", None),
        P("section", None, None, "sp"),
        P("section", None, None),
        P("section", "sp", None),
        P("section", None, "prompt", "sp"),
    )
    out_specs = (P("section", "prompt", "sp", None), P("section", None, "prompt", "sp"))
    return jax.shard_map(
        on_device, mesh=mesh, in_specs=in_specs, out_specs=out_specs, check_vma=False
    )
```
